32 devices in a mesh: ktot: 8 (over y, x, core), kvir: 4 (over z).
Axes of the slice: x: 2, y: 2, z: 4, core: 2. Of those that a mesh axis runs over, the one named last changes fastest.
Arguments:
- amplitudes: bfloat16 [8, 4, 672, 1024], P('ktot', 'kvir'), may hold values from -6 to 6
- ladder_integrals: bfloat16 [8, 4, 1024, 1024], P('ktot', 'kvir'), may hold values from -0.09375 to 0.09375
- listed: int32 [8, 4], P('ktot', 'kvir'), may hold values 0 or 1
- current: bfloat16 [8, 672, 1024], P('ktot', 'kvir'), may hold values from -3 to 3
- denominators: float32 [8, 672, 1024], P('ktot', 'kvir'), may hold values from 2 to 8
- cycle_integrals: bfloat16 [8, 512, 512], P('ktot', 'kvir'), may hold values from -0.25 to 0.25
Outputs:
- ladder_res: bfloat16 [8, 672, 1024], P('ktot', 'kvir')
- cycle_res: float32 [8, 1344, 1344], P('ktot', 'kvir')
The draws below stay inside these ranges and needn't reach their ends.
All inputs are finite; a program needn't handle non-finite values. No bound on the sum of `listed` on one device may be relied on, other than what follows from the above.
Results may differ from the reference program's by a relative error of at most 0.017.
Values may be sent and summed in bfloat16 or wider, within the bound.
A program may use at most 64 MiB of HBM per device.

```python
import math
import jax
import jax.numpy as jnp
from jax import lax

VV = 1024
ROWS = 672
NKT = 8
NKC = 4
CYCLE = 512
YR = 1344
N_KTOT = 8
N_KVIR = 4


def with_ends(drawn, stream_key, least, top_value):
    spot = [jax.random.randint(jax.random.fold_in(stream_key, axis), (), 0, length) for axis, length in enumerate(drawn.shape)]
    main_axis = drawn.shape.index(max(drawn.shape))
    beside = spot[:main_axis] + [(spot[main_axis] + 1) % drawn.shape[main_axis]] + spot[main_axis + 1:]
    return drawn.at[tuple(spot)].set(least).at[tuple(beside)].set(top_value)


def steps_of(stream_key, extent, shards, smallest, top_value):
    gain, own = 1.0, jax.random.fold_in(stream_key, 6)
    for position, shards_of in shards:
        heights = jnp.exp(jax.random.uniform(jax.random.fold_in(own, position), (shards_of,), jnp.float32, smallest / len(shards), top_value / len(shards)))
        gain = gain * jnp.repeat(heights, extent[position] // shards_of).reshape([-1 if axis == position else 1 for axis in range(len(extent))])
    return gain


def normal_values(rng, extent, deviation, limit, shards=(), held_as=jnp.bfloat16):
    result = jax.random.normal(rng, extent, jnp.float32) * deviation
    if len(shards) > 0:
        result = steps_of(rng, extent, shards, -0.22, 0.18) * result
    return jnp.clip(result, min=-limit, max=limit).astype(held_as)


def setup_inputs(seed: int = 0) -> dict:
    arg_keys = jax.random.split(jax.random.key(seed), 7)
    return {
        "amplitudes": normal_values(arg_keys[0], (NKT, NKC, ROWS, VV), 1.0, 6.0, ((0, 8), (1, 4))),
        "ladder_integrals": normal_values(arg_keys[1], (NKT, NKC, VV, VV), (VV * NKC) ** -0.5, 0.09375, ((0, 8), (1, 4))),
        "listed": with_ends((jax.random.randint(arg_keys[2], (NKT, NKC), 0, 4) < 3).astype(jnp.int32), jax.random.fold_in(arg_keys[2], 1), 0, 1),
        "current": normal_values(arg_keys[3], (NKT, ROWS, VV), 0.5, 3.0, ((0, 8), (1, 4))),
        "denominators": jnp.clip(jnp.exp(math.log(8.0) - 1.3862944 * jax.random.uniform(arg_keys[4], (NKT, ROWS, VV), jnp.float32) ** steps_of(arg_keys[4], (NKT, ROWS, VV), ((0, 8), (1, 4)), -0.2, 0.2)), 2.0, 8.0),
        "cycle_integrals": normal_values(arg_keys[5], (NKT, CYCLE, CYCLE), CYCLE ** -0.5, 0.25, ((0, 8), (1, 4))),
    }


def reference(amplitudes, ladder_integrals, listed, current, denominators, cycle_integrals):
    def per_total(inputs):
        amp_blocks, int_blocks, marks = inputs

        def per_contracted(running, item):
            amp_one, int_one, mark_one = item
            product = jnp.dot(amp_one, int_one, preferred_element_type=jnp.float32)
            return running + product * mark_one.astype(jnp.float32), None

        summed, unused = lax.scan(per_contracted, jnp.zeros((ROWS, VV), jnp.float32), (amp_blocks, int_blocks, marks))
        return summed

    ladder = lax.map(per_total, (amplitudes, ladder_integrals, listed))
    ladder_res = ladder.astype(jnp.bfloat16)
    updated = (current.astype(jnp.float32) + ladder / denominators).astype(jnp.bfloat16)
    row_share = ROWS // N_KVIR
    col_width = VV // N_KTOT
    cycle_matrix = updated.reshape(NKT, N_KVIR, row_share, NKT, col_width)
    cycle_matrix = cycle_matrix.transpose(3, 2, 0, 1, 4).reshape(NKT, YR, CYCLE)

    def per_transfer(inputs):
        cycle_block, cycle_weights = inputs
        column_parts = cycle_block.reshape(YR, N_KVIR, col_width).transpose(1, 0, 2)
        weight_parts = cycle_weights.reshape(N_KVIR, col_width, CYCLE)

        def add_part(running, item):
            column_one, weight_one = item
            partial_sum = jnp.dot(column_one, weight_one, preferred_element_type=jnp.float32)
            rounded = lax.optimization_barrier(partial_sum.astype(jnp.bfloat16))
            return running + rounded.astype(jnp.float32), None

        summed, unused = lax.scan(add_part, jnp.zeros((YR, CYCLE), jnp.float32), (column_parts, weight_parts))
        mixed = summed.astype(jnp.bfloat16)
        return jnp.dot(mixed, cycle_block.T, preferred_element_type=jnp.float32) * (CYCLE ** -0.5)

    cycle_res = lax.map(per_transfer, (cycle_matrix, cycle_integrals))
    return ladder_res, cycle_res
```

```python
import functools
import jax
import jax.numpy as jnp
from jax import lax
from jax.sharding import PartitionSpec as P
from jax.experimental import pallas as pl
from jax.experimental.pallas import tpu as pltpu

MESH = pl.DeviceIdType.MESH


def pieces_of(rows):
    for pieces in (3, 7, 2, 1):
        if rows % (8 * pieces) == 0:
            return pieces
    return 1


def kernel(
    nq, nv, nc,
    amp_ref, int_ref, mark_ref, cur_ref, den_ref, cyc_ref,
    lad_ref, out_ref,
    part, left, right, send_p, send_m, upd, got, mixbuf, cyc, full, weights,
    s_p, r_p, s_m, r_m, s_a, r_a, s_cr, s_cl, r_c, s_wr, s_wl, r_w,
):
    me = lax.axis_index("ktot")
    z = lax.axis_index("kvir")
    rc = cur_ref.shape[1]
    cw = upd.shape[3]
    has_left = z > 0
    has_right = z < nv - 1

    def peer(i):
        return lax.rem(me + i, nq)

    barrier = pltpu.get_barrier_semaphore()

    @pl.when(has_left)
    def _():
        pl.semaphore_signal(barrier, inc=1, device_id=(me, z - 1), device_id_type=MESH)

    @pl.when(has_right)
    def _():
        pl.semaphore_signal(barrier, inc=1, device_id=(me, z + 1), device_id_type=MESH)

    for i in range(1, nq):
        pl.semaphore_signal(barrier, inc=1, device_id=(peer(i), z), device_id_type=MESH)
    pl.semaphore_wait(
        barrier, nq - 1 + has_left.astype(jnp.int32) + has_right.astype(jnp.int32))

    def to(ref, there, send, recv, k, v):
        return pltpu.make_async_remote_copy(
            src_ref=ref, dst_ref=there, send_sem=send, recv_sem=recv,
            device_id=(k, v), device_id_type=MESH)

    def plus(d, j):
        return to(send_p.at[d, j], left.at[d, j], s_p.at[d, j], r_p.at[d, j], me, z + 1)

    def minus(d, j):
        return to(send_m.at[d, j], right.at[d, j], s_m.at[d, j], r_m.at[d, j], me, z - 1)

    def exchange(i, j):
        return to(upd.at[j, peer(i)], got.at[j, me], s_a.at[j, i], r_a.at[j, me], peer(i), z)

    def exchange_in(i, j):
        k = lax.rem(me + nq - i, nq)
        return to(upd.at[j, k], got.at[j, k], s_a.at[j, i], r_a.at[j, k], peer(i), z)

    def spread(v, j, right_way):
        rows = pl.ds(j * rc * nq, rc * nq)
        ref = cyc.at[v, rows]
        return to(ref, ref, (s_cr if right_way else s_cl).at[v, j], r_c.at[v, j], me,
                  z + 1 if right_way else z - 1)

    def wspread(v, right_way):
        ref = weights.at[v]
        return to(ref, ref, (s_wr if right_way else s_wl).at[v], r_w.at[v], me,
                  z + 1 if right_way else z - 1)

    def send_both(make):
        @pl.when(has_right)
        def _():
            make(True).start()

        @pl.when(has_left)
        def _():
            make(False).start()

    weights[z] = cyc_ref[...]
    send_both(lambda way: wspread(z, way))

    mark = mark_ref[0, 0].astype(jnp.float32)

    def ladder_block(i, carry):
        d = jnp.where(z < nv // 2, nv - 1 - i, i)
        part[d] = jnp.dot(amp_ref[d], int_ref[...], preferred_element_type=jnp.float32) * mark
        return carry

    lax.fori_loop(0, nv, ladder_block, 0)

    def mine(d, j):
        return part[d, j * rc:(j + 1) * rc, :]

    def reduce_plus(d, j):
        @pl.when(z == 0)
        def _():
            send_p[d, j] = mine(d, j).astype(jnp.bfloat16)

        @pl.when(has_left & (z < d))
        def _():
            plus(d, j).wait_recv()
            send_p[d, j] = (mine(d, j) + left[d, j].astype(jnp.float32)).astype(jnp.bfloat16)

        @pl.when(z < d)
        def _():
            plus(d, j).start()

    def reduce_minus(d, j):
        @pl.when(z == nv - 1)
        def _():
            send_m[d, j] = mine(d, j).astype(jnp.bfloat16)

        @pl.when(has_right & (z > d))
        def _():
            minus(d, j).wait_recv()
            send_m[d, j] = (mine(d, j) + right[d, j].astype(jnp.float32)).astype(jnp.bfloat16)

        @pl.when(z > d)
        def _():
            minus(d, j).start()

    def reduce(j):
        for i in range(nv - 1):
            reduce_plus(nv - 1 - i, j)
            reduce_minus(i, j)

    def finish(j):
        @pl.when(has_left)
        def _():
            plus(z, j).wait_recv()
            part[z, j * rc:(j + 1) * rc, :] += left[z, j].astype(jnp.float32)

        @pl.when(has_right)
        def _():
            minus(z, j).wait_recv()
            part[z, j * rc:(j + 1) * rc, :] += right[z, j].astype(jnp.float32)

        total = mine(z, j)
        lad_ref[j] = total.astype(jnp.bfloat16)
        new = (cur_ref[j].astype(jnp.float32) + total / den_ref[j]).astype(jnp.bfloat16)
        for q in range(nq):
            upd[j, q] = new[:, q * cw:(q + 1) * cw]
        for i in range(1, nq):
            exchange(i, j).start()
        got[j, me] = upd[j, me]

    def collect(j):
        for i in range(1, nq):
            exchange_in(i, j).wait_recv()
        for k in range(nq):
            mixbuf[pl.ds(k, rc, stride=nq), :] = got[j, k].astype(jnp.float32)
        cyc[z, j * rc * nq:(j + 1) * rc * nq, :] = mixbuf[...].astype(jnp.bfloat16)
        send_both(lambda way: spread(z, j, way))

    def pass_on(make):
        for h in range(1, nv):
            @pl.when(z - h >= 0)
            def _():
                make(z - h, True).wait_recv()

                @pl.when(has_right)
                def _():
                    make(z - h, True).start()

            @pl.when(z + h < nv)
            def _():
                make(z + h, False).wait_recv()

                @pl.when(has_left)
                def _():
                    make(z + h, False).start()

    for s in range(nc + 2):
        if s < nc:
            reduce(s)
        if s == 0:
            pass_on(wspread)
        if 0 <= s - 1 < nc:
            collect(s - 1)
        if s < nc:
            finish(s)
        if 0 <= s - 2 < nc:
            pass_on(lambda v, way: spread(v, s - 2, way))

    for v in range(nv):
        full[:, v * cw:(v + 1) * cw] = cyc[v]
    share = full.shape[0] // nv
    start = pl.multiple_of(z * share, share)
    mixed = jnp.zeros((share, cyc_ref.shape[1]), jnp.float32)
    for v in range(nv):
        term = jnp.dot(cyc[v, pl.ds(start, share), :], weights[v], preferred_element_type=jnp.float32)
        mixed = mixed + term.astype(jnp.bfloat16).astype(jnp.float32)
    result = lax.dot_general(
        mixed.astype(jnp.bfloat16), full[...], (((1,), (1,)), ((), ())),
        preferred_element_type=jnp.float32)
    out_ref[...] = result * cyc_ref.shape[1] ** (-0.5)

    for j in range(nc):
        for d in range(nv):
            @pl.when(z < d)
            def _():
                plus(d, j).wait_send()

            @pl.when(z > d)
            def _():
                minus(d, j).wait_send()
        for i in range(1, nq):
            exchange(i, j).wait_send()

    def drain(v, make):
        @pl.when((v <= z) & has_right)
        def _():
            make(v, True).wait_send()

        @pl.when((v >= z) & has_left)
        def _():
            make(v, False).wait_send()

    for v in range(nv):
        drain(v, wspread)
        for j in range(nc):
            drain(v, lambda v, way: spread(v, j, way))


def fused(nq, nv, amplitudes, ladder_integrals, listed, current, denominators, cycle_integrals):
    rows, width = current.shape[1:]
    cw = width // nq
    nc = pieces_of(rows)
    rc = rows // nc
    cycle = cycle_integrals.shape[2]
    yr = rows * nq
    b16, f32 = jnp.bfloat16, jnp.float32
    vmem = pl.BlockSpec(memory_space=pltpu.VMEM)
    dma = pltpu.SemaphoreType.DMA
    lad, out = pl.pallas_call(
        functools.partial(kernel, nq, nv, nc),
        out_shape=(jax.ShapeDtypeStruct((nc, rc, width), b16),
                   jax.ShapeDtypeStruct((yr // nv, yr), f32)),
        in_specs=[vmem, vmem, pl.BlockSpec(memory_space=pltpu.SMEM), vmem, vmem, vmem],
        out_specs=(vmem, vmem),
        scratch_shapes=[
            pltpu.VMEM((nv, rows, width), f32),
            pltpu.VMEM((nv, nc, rc, width), b16),
            pltpu.VMEM((nv, nc, rc, width), b16),
            pltpu.VMEM((nv, nc, rc, width), b16),
            pltpu.VMEM((nv, nc, rc, width), b16),
            pltpu.VMEM((nc, nq, rc, cw), b16),
            pltpu.VMEM((nc, nq, rc, cw), b16),
            pltpu.VMEM((rc * nq, cw), f32),
            pltpu.VMEM((nv, yr, cw), b16),
            pltpu.VMEM((yr, cw * nv), b16),
            pltpu.VMEM((nv, cycle // nv, cycle), b16),
            dma((nv, nc)), dma((nv, nc)), dma((nv, nc)), dma((nv, nc)),
            dma((nc, nq)), dma((nc, nq)),
            dma((nv, nc)), dma((nv, nc)), dma((nv, nc)),
            dma((nv,)), dma((nv,)), dma((nv,)),
        ],
        compiler_params=pltpu.CompilerParams(
            collective_id=0, has_side_effects=True, vmem_limit_bytes=56 * 2 ** 20),
    )(
        amplitudes.reshape(nv, rows, amplitudes.shape[3]),
        ladder_integrals[0, 0],
        listed,
        current.reshape(nc, rc, width),
        denominators.reshape(nc, rc, width),
        cycle_integrals[0],
    )
    return lad.reshape(1, rows, width), out[None]


def general(amplitudes, ladder_integrals, listed, current, denominators, cycle_integrals):
    mark = listed[0, 0].astype(jnp.float32)
    rows, width = current.shape[1:]
    nq = lax.axis_size("ktot")
    nv = lax.axis_size("kvir")
    partial = jnp.dot(amplitudes[0, 0], ladder_integrals[0, 0], preferred_element_type=jnp.float32)
    ladder = lax.psum_scatter(partial * mark, "kvir", scatter_dimension=0, tiled=True)
    updated = (current[0].astype(jnp.float32) + ladder / denominators[0]).astype(jnp.bfloat16)
    cw = width // nq
    received = lax.all_to_all(
        updated.reshape(rows, nq, cw), "ktot", split_axis=1, concat_axis=1, tiled=True)
    local = received.reshape(rows * nq, cw)
    weights = cycle_integrals[0]
    cycle = weights.shape[1]
    share = local.shape[0] // nv
    full = lax.all_gather(local, "kvir", axis=1, tiled=True)
    full_weights = lax.all_gather(weights, "kvir", axis=0, tiled=True)
    mine = lax.dynamic_slice_in_dim(full, lax.axis_index("kvir") * share, share, 0)
    terms = jnp.einsum(
        "svw,vwc->vsc", mine.reshape(share, nv, cw), full_weights.reshape(nv, cw, cycle),
        preferred_element_type=jnp.float32)
    terms = terms.astype(jnp.bfloat16).astype(jnp.float32)
    mixed = jnp.sum(terms, axis=0).astype(jnp.bfloat16)
    out = lax.dot_general(
        mixed, full, (((1,), (1,)), ((), ())), preferred_element_type=jnp.float32)
    return ladder.astype(jnp.bfloat16)[None], (out * cycle ** (-0.5))[None]


def solution(mesh):
    nq, nv = mesh.shape["ktot"], mesh.shape["kvir"]

    def shards(*arrays):
        rows, width = arrays[3].shape[1:]
        share = rows * nq // nv
        fits = (rows % 8 == 0 and width % (128 * nq) == 0 and share % 16 == 0
                and arrays[5].shape[2] == width // nq * nv
                and rows * nv == arrays[0].shape[2])
        return fused(nq, nv, *arrays) if fits else general(*arrays)

    return jax.shard_map(
        shards,
        mesh=mesh,
        in_specs=(
            P("ktot", "kvir", None, None),
            P("ktot", "kvir", None, None),
            P("ktot", "kvir"),
            P("ktot", "kvir", None),
            P("ktot", "kvir", None),
            P("ktot", "kvir", None),
        ),
        out_specs=(P("ktot", "kvir", None), P("ktot", "kvir", None)),
        check_vma=False,
    )
```

```python
import functools
import jax
import jax.numpy as jnp
from jax import lax
from jax.sharding import PartitionSpec as P
from jax.experimental import pallas as pl
from jax.experimental.pallas import tpu as pltpu

LAGS = (1, 1, 2, 3)
MESH = pl.DeviceIdType.MESH


def pieces_of(rows):
    for pieces in (3, 7, 2, 1):
        if rows % (8 * pieces) == 0:
            return pieces
    return 1


def kernel(
    nq, nv, nc,
    amp_ref, int_ref, mark_ref, cur_ref, den_ref, cyc_ref,
    lad_ref, out_ref,
    part, left, right, send_p, send_m, upd, got, mixbuf, cyc, full, weights,
    s_p, r_p, s_m, r_m, s_a, r_a, s_cr, s_cl, r_c, s_wr, s_wl, r_w,
):
    me = lax.axis_index("ktot")
    z = lax.axis_index("kvir")
    rc = cur_ref.shape[1]
    cw = upd.shape[3]
    has_left = z > 0
    has_right = z < nv - 1
    inner = has_left & has_right
    low = z < nv // 2

    def peer(i):
        return lax.rem(me + i, nq)

    barrier = pltpu.get_barrier_semaphore()

    @pl.when(has_left)
    def _():
        pl.semaphore_signal(barrier, inc=1, device_id=(me, z - 1), device_id_type=MESH)

    @pl.when(has_right)
    def _():
        pl.semaphore_signal(barrier, inc=1, device_id=(me, z + 1), device_id_type=MESH)

    for i in range(1, nq):
        pl.semaphore_signal(barrier, inc=1, device_id=(peer(i), z), device_id_type=MESH)
    pl.semaphore_wait(
        barrier, nq - 1 + has_left.astype(jnp.int32) + has_right.astype(jnp.int32))

    def to(ref, there, send, recv, k, v):
        return pltpu.make_async_remote_copy(
            src_ref=ref, dst_ref=there, send_sem=send, recv_sem=recv,
            device_id=(k, v), device_id_type=MESH)

    def plus(d, j):
        return to(send_p.at[d, j], left.at[d, j], s_p.at[d, j], r_p.at[d, j], me, z + 1)

    def minus(d, j):
        return to(send_m.at[d, j], right.at[d, j], s_m.at[d, j], r_m.at[d, j], me, z - 1)

    def exchange(i, j):
        return to(upd.at[j, peer(i)], got.at[j, me], s_a.at[j, i], r_a.at[j, me], peer(i), z)

    def exchange_in(i, j):
        k = lax.rem(me + nq - i, nq)
        return to(upd.at[j, k], got.at[j, k], s_a.at[j, i], r_a.at[j, k], peer(i), z)

    def spread(v, j, right_way):
        rows = pl.ds(j * rc * nq, rc * nq)
        ref = cyc.at[v, rows]
        return to(ref, ref, (s_cr if right_way else s_cl).at[v, j], r_c.at[v, j], me,
                  z + 1 if right_way else z - 1)

    def wspread(v, right_way):
        ref = weights.at[v]
        return to(ref, ref, (s_wr if right_way else s_wl).at[v], r_w.at[v], me,
                  z + 1 if right_way else z - 1)

    def send_both(make):
        @pl.when(has_right)
        def _():
            make(True).start()

        @pl.when(has_left)
        def _():
            make(False).start()

    weights[z] = cyc_ref[...]
    send_both(lambda way: wspread(z, way))

    mark = mark_ref[0, 0].astype(jnp.float32)

    def mine(d, j):
        return part[d, j * rc:(j + 1) * rc, :]

    def end_send(d, j):
        @pl.when((z == 0) & (d > 0))
        def _():
            send_p[d, j] = mine(d, j).astype(jnp.bfloat16)
            plus(d, j).start()

        @pl.when((z == nv - 1) & (d < nv - 1))
        def _():
            send_m[d, j] = mine(d, j).astype(jnp.bfloat16)
            minus(d, j).start()

    def ladder_block(i, carry):
        d = jnp.where(low, nv - 1 - i, i)
        part[d] = jnp.dot(amp_ref[d], int_ref[...], preferred_element_type=jnp.float32) * mark
        end_send(d, 0)
        return carry

    lax.fori_loop(0, nv, ladder_block, 0)

    def reduce_plus(d, j):
        plus(d, j).wait_recv()
        send_p[d, j] = (mine(d, j) + left[d, j].astype(jnp.float32)).astype(jnp.bfloat16)
        plus(d, j).start()

    def reduce_minus(d, j):
        minus(d, j).wait_recv()
        send_m[d, j] = (mine(d, j) + right[d, j].astype(jnp.float32)).astype(jnp.bfloat16)
        minus(d, j).start()

    def reduce(j, near):
        up = inner & (low if near else jnp.logical_not(low))
        down = inner & (jnp.logical_not(low) if near else low)
        for i in range(nv - 1):
            p, m = nv - 1 - i, i

            @pl.when(up & (z < p))
            def _():
                reduce_plus(p, j)

            @pl.when(down & (z > m))
            def _():
                reduce_minus(m, j)

    def finish(j):
        @pl.when(has_left)
        def _():
            plus(z, j).wait_recv()
            part[z, j * rc:(j + 1) * rc, :] += left[z, j].astype(jnp.float32)

        @pl.when(has_right)
        def _():
            minus(z, j).wait_recv()
            part[z, j * rc:(j + 1) * rc, :] += right[z, j].astype(jnp.float32)

        total = mine(z, j)
        lad_ref[j] = total.astype(jnp.bfloat16)
        new = (cur_ref[j].astype(jnp.float32) + total / den_ref[j]).astype(jnp.bfloat16)
        for q in range(nq):
            upd[j, q] = new[:, q * cw:(q + 1) * cw]
        for i in range(1, nq):
            exchange(i, j).start()
        got[j, me] = upd[j, me]

    def collect(j):
        for i in range(1, nq):
            exchange_in(i, j).wait_recv()
        for k in range(nq):
            mixbuf[pl.ds(k, rc, stride=nq), :] = got[j, k].astype(jnp.float32)
        cyc[z, j * rc * nq:(j + 1) * rc * nq, :] = mixbuf[...].astype(jnp.bfloat16)
        send_both(lambda way: spread(z, j, way))

    def pass_on(make, wanted):
        for h in range(1, nv):
            @pl.when(wanted(z - h) & (z - h >= 0))
            def _():
                make(z - h, True).wait_recv()

                @pl.when(has_right)
                def _():
                    make(z - h, True).start()

            @pl.when(wanted(z + h) & (z + h < nv))
            def _():
                make(z + h, False).wait_recv()

                @pl.when(has_left)
                def _():
                    make(z + h, False).start()

    def from_inner(v):
        return inner & (v > 0) & (v < nv - 1)

    def from_end(near):
        def wanted(v):
            return inner & jnp.where(low == near, v == 0, v == nv - 1)
        return wanted

    def at_end(v):
        return jnp.logical_not(inner) & (v == v)

    for j in range(1, nc):
        for i in range(1, nv):
            end_send(jnp.where(low, nv - i, i - 1), j)

    far, closing, gathering, passing = LAGS
    for s in range(nc + passing):
        if s < nc:
            reduce(s, True)
        if s == 0:
            pass_on(wspread, lambda v: inner & (v == v))
        if 0 <= s - gathering < nc:
            collect(s - gathering)
        if 0 <= s - far < nc:
            reduce(s - far, False)
        if 0 <= s - closing < nc:
            finish(s - closing)
        if 0 <= s - passing < nc:
            pass_on(lambda v, way: spread(v, s - passing, way), from_inner)
    for s in range(nc + far):
        if s < nc:
            pass_on(lambda v, way: spread(v, s, way), from_end(True))
        if 0 <= s - far < nc:
            pass_on(lambda v, way: spread(v, s - far, way), from_end(False))
    pass_on(wspread, at_end)
    for j in range(nc):
        pass_on(lambda v, way: spread(v, j, way), at_end)

    for v in range(nv):
        full[:, v * cw:(v + 1) * cw] = cyc[v]
    share = full.shape[0] // nv
    start = pl.multiple_of(z * share, share)
    mixed = jnp.zeros((share, cyc_ref.shape[1]), jnp.float32)
    for v in range(nv):
        term = jnp.dot(cyc[v, pl.ds(start, share), :], weights[v], preferred_element_type=jnp.float32)
        mixed = mixed + term.astype(jnp.bfloat16).astype(jnp.float32)
    result = lax.dot_general(
        mixed.astype(jnp.bfloat16), full[...], (((1,), (1,)), ((), ())),
        preferred_element_type=jnp.float32)
    out_ref[...] = result * cyc_ref.shape[1] ** (-0.5)

    for j in range(nc):
        for d in range(nv):
            @pl.when(z < d)
            def _():
                plus(d, j).wait_send()

            @pl.when(z > d)
            def _():
                minus(d, j).wait_send()
        for i in range(1, nq):
            exchange(i, j).wait_send()

    def drain(v, make):
        @pl.when((v <= z) & has_right)
        def _():
            make(v, True).wait_send()

        @pl.when((v >= z) & has_left)
        def _():
            make(v, False).wait_send()

    for v in range(nv):
        drain(v, wspread)
        for j in range(nc):
            drain(v, lambda v, way: spread(v, j, way))


def fused(nq, nv, amplitudes, ladder_integrals, listed, current, denominators, cycle_integrals):
    rows, width = current.shape[1:]
    cw = width // nq
    nc = pieces_of(rows)
    rc = rows // nc
    cycle = cycle_integrals.shape[2]
    yr = rows * nq
    b16, f32 = jnp.bfloat16, jnp.float32
    vmem = pl.BlockSpec(memory_space=pltpu.VMEM)
    dma = pltpu.SemaphoreType.DMA
    lad, out = pl.pallas_call(
        functools.partial(kernel, nq, nv, nc),
        out_shape=(jax.ShapeDtypeStruct((nc, rc, width), b16),
                   jax.ShapeDtypeStruct((yr // nv, yr), f32)),
        in_specs=[vmem, vmem, pl.BlockSpec(memory_space=pltpu.SMEM), vmem, vmem, vmem],
        out_specs=(vmem, vmem),
        scratch_shapes=[
            pltpu.VMEM((nv, rows, width), f32),
            pltpu.VMEM((nv, nc, rc, width), b16),
            pltpu.VMEM((nv, nc, rc, width), b16),
            pltpu.VMEM((nv, nc, rc, width), b16),
            pltpu.VMEM((nv, nc, rc, width), b16),
            pltpu.VMEM((nc, nq, rc, cw), b16),
            pltpu.VMEM((nc, nq, rc, cw), b16),
            pltpu.VMEM((rc * nq, cw), f32),
            pltpu.VMEM((nv, yr, cw), b16),
            pltpu.VMEM((yr, cw * nv), b16),
            pltpu.VMEM((nv, cycle // nv, cycle), b16),
            dma((nv, nc)), dma((nv, nc)), dma((nv, nc)), dma((nv, nc)),
            dma((nc, nq)), dma((nc, nq)),
            dma((nv, nc)), dma((nv, nc)), dma((nv, nc)),
            dma((nv,)), dma((nv,)), dma((nv,)),
        ],
        compiler_params=pltpu.CompilerParams(
            collective_id=0, has_side_effects=True, vmem_limit_bytes=56 * 2 ** 20),
    )(
        amplitudes.reshape(nv, rows, amplitudes.shape[3]),
        ladder_integrals[0, 0],
        listed,
        current.reshape(nc, rc, width),
        denominators.reshape(nc, rc, width),
        cycle_integrals[0],
    )
    return lad.reshape(1, rows, width), out[None]


def general(amplitudes, ladder_integrals, listed, current, denominators, cycle_integrals):
    mark = listed[0, 0].astype(jnp.float32)
    rows, width = current.shape[1:]
    nq = lax.axis_size("ktot")
    nv = lax.axis_size("kvir")
    partial = jnp.dot(amplitudes[0, 0], ladder_integrals[0, 0], preferred_element_type=jnp.float32)
    ladder = lax.psum_scatter(partial * mark, "kvir", scatter_dimension=0, tiled=True)
    updated = (current[0].astype(jnp.float32) + ladder / denominators[0]).astype(jnp.bfloat16)
    cw = width // nq
    received = lax.all_to_all(
        updated.reshape(rows, nq, cw), "ktot", split_axis=1, concat_axis=1, tiled=True)
    local = received.reshape(rows * nq, cw)
    weights = cycle_integrals[0]
    cycle = weights.shape[1]
    share = local.shape[0] // nv
    full = lax.all_gather(local, "kvir", axis=1, tiled=True)
    full_weights = lax.all_gather(weights, "kvir", axis=0, tiled=True)
    mine = lax.dynamic_slice_in_dim(full, lax.axis_index("kvir") * share, share, 0)
    terms = jnp.einsum(
        "svw,vwc->vsc", mine.reshape(share, nv, cw), full_weights.reshape(nv, cw, cycle),
        preferred_element_type=jnp.float32)
    terms = terms.astype(jnp.bfloat16).astype(jnp.float32)
    mixed = jnp.sum(terms, axis=0).astype(jnp.bfloat16)
    out = lax.dot_general(
        mixed, full, (((1,), (1,)), ((), ())), preferred_element_type=jnp.float32)
    return ladder.astype(jnp.bfloat16)[None], (out * cycle ** (-0.5))[None]


def solution(mesh):
    nq, nv = mesh.shape["ktot"], mesh.shape["kvir"]

    def shards(*arrays):
        rows, width = arrays[3].shape[1:]
        share = rows * nq // nv
        fits = (rows % 8 == 0 and width % (128 * nq) == 0 and share % 16 == 0
                and arrays[5].shape[2] == width // nq * nv
                and rows * nv == arrays[0].shape[2])
        return fused(nq, nv, *arrays) if fits else general(*arrays)

    return jax.shard_map(
        shards,
        mesh=mesh,
        in_specs=(
            P("ktot", "kvir", None, None),
            P("ktot", "kvir", None, None),
            P("ktot", "kvir"),
            P("ktot", "kvir", None),
            P("ktot", "kvir", None),
            P("ktot", "kvir", None),
        ),
        out_specs=(P("ktot", "kvir", None), P("ktot", "kvir", None)),
        check_vma=False,
    )
```
